256 devices in a mesh: section: 2 (over z_lo), dp: 16 (over y, z_hi), tensor: 8 (over x, core).
Axes of the slice: x: 4, y: 4, z: 8 (z_hi: 4, z_lo: 2; z = z_hi * 2 + z_lo), core: 2. Of those that a mesh axis runs over, the one named last changes fastest.
Arguments:
- outgoing: bfloat16 [2, 32768, 8192], P('section', 'dp', 'tensor'), may hold values from -6 to 6
- embedding: bfloat16 [64256, 8192], P(('section', 'dp'), 'tensor'), may hold values from -3 to 3
- shared_basis: bfloat16 [8192, 512], P('tensor'), may hold values from -0.0625 to 0.0625
- token_ids: int32 [2, 32768], P('section', 'dp'), may hold values from 0 to 64255, as said below
- row_route: int32 [2, 32768], P('section', 'dp'), may hold values from 0 to 32767, as said below
Outputs:
- lifted: bfloat16 [2, 32768, 8192], P('section', 'dp', 'tensor')
The draws below stay inside these ranges and needn't reach their ends.
Inputs may be any that keep to these rules, and one draw needn't show every extreme that they name: row_route[0] is a permutation of the 32768 rows and row_route[1] is its inverse; the 2048 rows of one dp index in one section go to exactly 2048 / 16 rows of each dp index in the other section. token_ids[1, row_route[0, r]] = token_ids[0, r]; the 2048 rows of one dp index in either section name each of the 32 aligned vocabulary blocks of 2008 ids exactly 2048 / 32 times.
All inputs are finite; a program needn't handle non-finite values.
Results may differ from the reference program's by a relative error of at most 0.0044.
Values may be sent and summed in bfloat16 or wider, within the bound.
A program may use at most 64 MiB of HBM per device.

```python
import jax
import jax.numpy as jnp
from jax import lax

D = 8192
R = 512
VOCAB = 64256
TOK_DEV = 2048
TOKENS = 32768
OWNERS = 32


def permute_each(key, count):

    def one_perm(sub_key):
        return jax.random.permutation(sub_key, TOK_DEV).astype(jnp.int32)
    return jax.vmap(one_perm)(jax.random.split(key, count))


def layout_tables(key):
    dp_count = TOKENS // TOK_DEV
    per_owner = TOK_DEV // OWNERS
    vocab_block = VOCAB // OWNERS
    keys = jax.random.split(key, 4)
    entries = jnp.arange(TOK_DEV, dtype=jnp.int32)
    owner_of = entries // per_owner
    within_owner = entries % per_owner
    sources = jnp.arange(dp_count, dtype=jnp.int32)[:, None]
    shifts = jax.random.randint(keys[0], (2,), 0, dp_count).astype(jnp.int32)
    target_dp = (sources + owner_of[None, :] + within_owner[None, :] + shifts[owner_of // dp_count][None, :]) % dp_count
    row_perm = permute_each(keys[1], dp_count)
    source_rows = (sources * TOK_DEV + row_perm).reshape(-1)
    grid_index = (sources * TOK_DEV + entries[None, :]).reshape(-1)
    sort_keys = target_dp.reshape(-1) * TOKENS + grid_index
    sorted_entries = jnp.argsort(sort_keys).astype(jnp.int32)
    slots = jnp.zeros((TOKENS,), jnp.int32).at[sorted_entries].set(jnp.arange(TOKENS, dtype=jnp.int32))
    dest_perm = permute_each(keys[2], dp_count)
    dest_dp = slots // TOK_DEV
    positions = dest_dp * TOK_DEV + dest_perm[dest_dp, slots % TOK_DEV]
    first_route = jnp.zeros((TOKENS,), jnp.int32).at[source_rows].set(positions)
    second_route = jnp.zeros((TOKENS,), jnp.int32).at[first_route].set(jnp.arange(TOKENS, dtype=jnp.int32))
    offsets = jax.random.randint(keys[3], (dp_count, TOK_DEV), 0, vocab_block).astype(jnp.int32)
    grid_ids = owner_of[None, :] * vocab_block + offsets
    first_ids = jnp.zeros((TOKENS,), jnp.int32).at[source_rows].set(grid_ids.reshape(-1))
    second_ids = jnp.zeros((TOKENS,), jnp.int32).at[first_route].set(first_ids)
    return (jnp.stack([first_ids, second_ids]), jnp.stack([first_route, second_route]))


def draw_token_ids(key, part):
    tables = layout_tables(key)
    return tables[0]


def draw_row_route(key, part):
    tables = layout_tables(key)
    return tables[1]


def steps_of(own_key, shape, pieces, smallest, largest):
    def one(axis_at, blocks):
        draws = jax.random.uniform(jax.random.fold_in(jax.random.fold_in(own_key, 6), axis_at), (blocks,), jnp.float32, smallest / len(pieces), largest / len(pieces))
        return jnp.repeat(jnp.exp(draws), shape[axis_at] // blocks).reshape((-1,) + (1,) * (len(shape) - axis_at - 1))

    factor_of = one(*pieces[0])
    for cut in pieces[1:]:
        factor_of = factor_of * one(*cut)
    return factor_of


def gaussian(stream_key, extent, spread, most, pieces=(), held_as=jnp.bfloat16):
    array = spread * jax.random.normal(stream_key, extent, jnp.float32)
    if pieces:
        array = array * steps_of(stream_key, extent, pieces, -0.22, 0.18)
    return jnp.clip(array, -most, most).astype(held_as)


def setup_inputs(seed: int = 0) -> dict:
    arg_keys = jax.random.split(jax.random.key(seed), 6)
    outgoing = gaussian(arg_keys[0], (2, TOKENS, D), 1.0, 6.0, ((0, 2), (1, 16), (2, 8)))
    embedding = gaussian(arg_keys[1], (VOCAB, D), 0.5, 3.0, ((0, 32), (1, 8)))
    shared_basis = gaussian(arg_keys[2], (D, R), D ** -0.5, 0.0625, ((0, 8),))
    token_ids = draw_token_ids(jax.random.fold_in(arg_keys[5], 71), 0)
    row_route = draw_row_route(jax.random.fold_in(arg_keys[5], 71), 0)
    return dict(outgoing=outgoing, embedding=embedding, shared_basis=shared_basis, token_ids=token_ids, row_route=row_route)


def project_section(activations, section_ids, embedding, shared_basis, keep_embed):
    act_blocks = activations.reshape(-1, TOK_DEV, D)
    id_blocks = section_ids.reshape(-1, TOK_DEV)

    def project_block(inputs):
        block_acts, block_ids = inputs
        embed_term = embedding[block_ids].astype(jnp.float32)
        boundary = (block_acts.astype(jnp.float32) - keep_embed * embed_term).astype(jnp.bfloat16)
        return jnp.dot(boundary, shared_basis, preferred_element_type=jnp.float32).astype(jnp.bfloat16)

    return lax.map(project_block, (act_blocks, id_blocks)).reshape(TOKENS, R)


def lift_section(received, section_ids, embedding, shared_basis, keep_embed):
    coef_blocks = received.reshape(-1, TOK_DEV, R)
    id_blocks = section_ids.reshape(-1, TOK_DEV)

    def lift_block(inputs):
        block_coef, block_ids = inputs
        spanned = lax.dot_general(block_coef, shared_basis, (((1,), (1,)), ((), ())), preferred_element_type=jnp.float32)
        return (spanned + keep_embed * embedding[block_ids].astype(jnp.float32)).astype(jnp.bfloat16)

    return lax.map(lift_block, (coef_blocks, id_blocks)).reshape(TOKENS, D)


def reference(outgoing, embedding, shared_basis, token_ids, row_route):
    first_coef = project_section(outgoing[0], token_ids[0], embedding, shared_basis, 1.0)
    second_coef = project_section(outgoing[1], token_ids[1], embedding, shared_basis, 0.0)
    into_second = jnp.zeros((TOKENS, R), jnp.bfloat16).at[row_route[0]].set(first_coef)
    into_first = jnp.zeros((TOKENS, R), jnp.bfloat16).at[row_route[1]].set(second_coef)
    first_lift = lift_section(into_first, token_ids[0], embedding, shared_basis, 0.0)
    second_lift = lift_section(into_second, token_ids[1], embedding, shared_basis, 1.0)
    return jnp.stack([first_lift, second_lift])
```

```python
import jax
import jax.numpy as jnp
from jax import lax
from jax.experimental import pallas as pl
from jax.experimental.pallas import tpu as pltpu
from jax.sharding import PartitionSpec as P

BF16, F32, I32 = jnp.bfloat16, jnp.float32, jnp.int32
TOK = 2048
FEAT = 1024
RANK = 512
VBLOCK = 2008
LANES = 128
HALF = 1024
VWHOLE = 1920
EARLY = 12


def kernel(acts_hbm, emb_hbm, basis_hbm, ids_ref, route_ref, out_hbm,
           acts, emb, emb_tail, basis, looked, arrived, total, place_e,
           keys, key_col, rank_col, recv_col, send_row, ask, ask_in, ask_col,
           part, core_in, x_in, epart, ecore_in, ex_in,
           slots, coef_in, ebs, eb_in, gathered, coefs,
           load_sem, ask_s, ask_r, emb_s, emb_r, core_s, core_r, x_s, x_r,
           ecore_s, ecore_r, ex_s, ex_r, coef_s, coef_r, eb_s, eb_r,
           ag_s, ag_r, fwd_s, fwd_r, out_s):
    s = lax.axis_index("section")
    d = lax.axis_index("dp")
    t = lax.axis_index("tensor")
    y, zh, x, c = d // 4, d % 4, t // 2, t % 2

    def dev(s_, d_, t_):
        return {"section": s_, "dp": d_, "tensor": t_}

    def remote(src, dst, send_sem, recv_sem, to):
        return pltpu.make_async_remote_copy(
            src, dst, send_sem, recv_sem, device_id=to, device_id_type=pl.DeviceIdType.MESH)

    partner = dev(s, d, x * 2 + 1 - c)

    def dest(k):
        return (y + ((k % 4) + 2)) % 4 * 4 + (zh + ((k // 4) + 2)) % 4

    def source(k):
        return (y + 6 - (k % 4)) % 4 * 4 + (zh + 6 - (k // 4)) % 4

    def loop(n, body, start=0):
        def step(i, carry):
            body(i)
            return carry
        lax.fori_loop(start, n, step, 0)

    lane = lax.broadcasted_iota(I32, (LANES, LANES), 1)
    sub = lax.broadcasted_iota(I32, (LANES, LANES), 0)

    load_basis = pltpu.make_async_copy(basis_hbm, basis, load_sem.at[0])
    load_acts = pltpu.make_async_copy(acts_hbm, acts, load_sem.at[1])
    load_emb = pltpu.make_async_copy(emb_hbm, emb, load_sem.at[2])
    load_basis.start()
    load_acts.start()
    load_emb.start()

    barrier = pltpu.get_barrier_semaphore()

    def greet(to):
        pl.semaphore_signal(barrier, inc=1, device_id=to, device_id_type=pl.DeviceIdType.MESH)

    greet(partner)
    loop(4, lambda j: greet(dev(s, d, (x + j) % 4 * 2 + c)), 1)
    loop(16, lambda i: greet(dev(1 - s, (d + i) % 16, t)))

    @pl.when(s == 1)
    def _():
        loop(16, lambda i: greet(dev(s, (d + i) % 16, t)), 1)

    def column(row):
        return jnp.transpose(jnp.broadcast_to(row, (LANES, LANES)))

    def rank_of_columns(dst):
        def block(b):
            own = column(keys[pl.ds(b, 1), :])
            count = jnp.zeros((LANES, LANES), F32)
            for m in range(16):
                count += jnp.where(keys[m:m + 1, :] < own, 1.0, 0.0)
            rank = jnp.sum(count, axis=1, keepdims=True).astype(I32)
            dst[pl.ds(b * LANES, LANES), :] = jnp.broadcast_to(rank, (LANES, LANES))
        loop(16, block)

    pos16 = (lax.broadcasted_iota(I32, (16, LANES), 0) * LANES
             + lax.broadcasted_iota(I32, (16, LANES), 1))

    @pl.when(s == 1)
    def _():
        keys[...] = ids_ref[...] * TOK + pos16
        rank_of_columns(rank_col)

        def id_column(b):
            key_col[pl.ds(b * LANES, LANES), :] = column(ids_ref[pl.ds(b, 1), :])
        loop(16, id_column)

        def request(m):
            found = jnp.zeros((LANES, LANES), I32)
            for b in range(16):
                rows = slice(b * LANES, (b + 1) * LANES)
                found += jnp.where(rank_col[rows, :] == lane + m * LANES, key_col[rows, :], 0)
            ids = jnp.sum(found.astype(F32), axis=0, keepdims=True).astype(I32)
            ask[m] = jnp.broadcast_to(ids, (8, LANES))
        loop(16, request)

    load_basis.wait()
    load_acts.wait()

    def pack(top, bottom, dst, rows):
        n = top.shape[0]
        left = lax.broadcasted_iota(I32, (n, LANES), 1) < 64
        for g in range(4):
            cols = slice(g * LANES, (g + 1) * LANES)
            a, b = top[:, cols], bottom[:, cols]
            dst[0, g, rows, :] = jnp.where(left, a, pltpu.roll(b, 64, 1))
            dst[1, g, rows, :] = jnp.where(left, pltpu.roll(a, 64, 1), b)

    def project(i):
        top = jnp.dot(acts[pl.ds(i * 256, 256), :], basis[...], preferred_element_type=F32)
        bottom = jnp.dot(acts[pl.ds(HALF + i * 256, 256), :], basis[...], preferred_element_type=F32)
        pack(top, bottom, part, pl.ds(i * 256, 256))
    loop(4, project)

    pl.semaphore_wait(barrier, 4 + 16 + 15 * s)

    def ask_owner(i):
        k, so = i // 2, i % 2
        od = source(k)
        src, dst = ask.at[so * 8 + od // 2], ask_in.at[k]

        @pl.when((so == 1) & (od == d))
        def _():
            pltpu.make_async_copy(src, dst, ask_r.at[k]).start()

        @pl.when((so != 1) | (od != d))
        def _():
            remote(src, dst, ask_s.at[i], ask_r.at[k], dev(so, od, t)).start()

    @pl.when(s == 1)
    def _():
        loop(32, ask_owner)

    core_copy = remote(part.at[1 - c], core_in, core_s, core_r, partner)
    core_copy.start()

    load_emb.wait()
    emb_tail[...] = jnp.zeros_like(emb_tail)
    emb_tail[0:VBLOCK - VWHOLE, :] = emb[VWHOLE:VBLOCK, :]
    first_id = (s * 16 + d) * VBLOCK

    def emb_copy(k):
        return remote(looked.at[pl.ds(k * 64, 64)], arrived.at[pl.ds((2 * k + s) * 64, 64)],
                      emb_s.at[k], emb_r.at[2 * k + s], dev(1, dest(k), t))

    def is_self(k):
        return (s == 1) & (dest(k) == d)

    def send_rows(k):
        @pl.when(is_self(k))
        def _():
            pltpu.make_async_copy(looked.at[pl.ds(k * 64, 64)], arrived.at[pl.ds((2 * k + s) * 64, 64)],
                                  emb_r.at[2 * k + s]).start()

        @pl.when(jnp.logical_not(is_self(k)))
        def _():
            emb_copy(k).start()

    def look_up(i):
        for q in range(2):
            k = 2 * i + q
            pltpu.make_async_copy(ask_in.at[k], ask_in.at[k], ask_r.at[k]).wait()
            ask_col[...] = column(ask_in[k, 0:1, :])
            key_col[q * 64:(q + 1) * 64, :] = ask_col[pl.ds((d % 2) * 64, 64), :] - first_id
        want = key_col[0:LANES, :]
        hot = jnp.concatenate(
            [jnp.where(want == lane + m * LANES, 1.0, 0.0).astype(BF16) for m in range(16)], axis=1)
        rows = jnp.dot(hot[:, :VWHOLE], emb[0:VWHOLE, :], preferred_element_type=F32)
        rows += jnp.dot(hot[:, VWHOLE:], emb_tail[...], preferred_element_type=F32)
        looked[pl.ds(i * LANES, LANES), :] = rows.astype(BF16)

    def serve(i):
        look_up(i)
        send_rows(2 * i)
        send_rows(2 * i + 1)
    loop(4, serve)

    core_copy.wait()

    def x_copy(j):
        to = (x + j) % 4
        return remote(part.at[c, to], x_in.at[j - 1], x_s.at[j - 1], x_r.at[j - 1], dev(s, d, to * 2 + c))

    def add_core(j):
        to = (x + j) % 4
        part[c, to] = part[c, to] + core_in[to]

        @pl.when(j < 4)
        def _():
            x_copy(j).start()
    loop(5, add_core, 1)

    loop(EARLY // 2, serve, 4)
    loop(8, look_up, EARLY // 2)

    def project_rows(i):
        h = jnp.dot(looked[pl.ds(i * 256, 256), :], basis[...], preferred_element_type=F32)
        h = h.reshape(4, 2, 32, RANK)
        pack(h[:, 0].reshape(LANES, RANK), h[:, 1].reshape(LANES, RANK), epart, pl.ds(i * LANES, LANES))
    loop(4, project_rows)
    ecore_copy = remote(epart.at[1 - c], ecore_in, ecore_s, ecore_r, partner)
    ecore_copy.start()

    keys[...] = route_ref[...] - route_ref[...] % TOK + pos16

    def send_column(b):
        key_col[pl.ds(b * LANES, LANES), :] = column(keys[pl.ds(b, 1), :])
    loop(16, send_column)

    def send_rank(m):
        own = keys[pl.ds(m, 1), :]
        count = jnp.zeros((LANES, LANES), F32)
        for b in range(16):
            count += jnp.where(key_col[b * LANES:(b + 1) * LANES, :] < own, 1.0, 0.0)
        send_row[pl.ds(m, 1), :] = jnp.sum(count, axis=0, keepdims=True).astype(I32)
    loop(16, send_rank)

    ecore_copy.wait()

    def ex_copy(j):
        to = (x + j) % 4
        return remote(epart.at[c, to], ex_in.at[j - 1], ex_s.at[j - 1], ex_r.at[j - 1], dev(s, d, to * 2 + c))

    def add_ecore(j):
        to = (x + j) % 4
        epart[c, to] = epart[c, to] + ecore_in[to]

        @pl.when(j < 4)
        def _():
            ex_copy(j).start()
    loop(5, add_ecore, 1)

    keys[...] = route_ref[...]
    rank_of_columns(recv_col)

    @pl.when(s == 1)
    def _():
        def place(b):
            p = rank_col[pl.ds(b * LANES, LANES), :]
            o = p // 64
            k = ((zh + 4 - o % 4 + 2) % 4) * 4 + (y + 4 - (o // 4) % 4 + 2) % 4
            code = (2 * k + o // 16) * 64 + p % 64
            for m in range(16):
                place_e[pl.ds(b * LANES, LANES), m * LANES:(m + 1) * LANES] = (
                    jnp.where(code == lane + m * LANES, 1.0, 0.0).astype(BF16))
        loop(16, place)

    loop(4, lambda j: x_copy(j).wait(), 1)
    mine = (part[c, x] + x_in[0] + x_in[1] + x_in[2]).astype(BF16).astype(F32)
    half_left = lax.broadcasted_iota(I32, (HALF, LANES), 1) < 64
    unpacked = jnp.concatenate([mine, pltpu.roll(mine, 64, 1)], axis=0).astype(BF16)
    coefs[:, 0:LANES] = unpacked

    def order(b):
        hot = jnp.concatenate(
            [jnp.where(send_row[m:m + 1, :] == sub + b * LANES, 1.0, 0.0).astype(BF16)
             for m in range(16)], axis=1)
        rows = jnp.dot(hot, coefs[:, 0:LANES], preferred_element_type=F32)
        packed = jnp.where(lane[0:64] < 64, rows[0:64], pltpu.roll(rows[64:128], 64, 1))
        slots[pl.ds(b * 64, 64), :] = packed.astype(BF16)
    loop(16, order)

    def coef_copy(i):
        to = (d + i) % 16
        return remote(slots.at[pl.ds(to * 64, 64)], coef_in.at[pl.ds(d * 64, 64)],
                      coef_s.at[i], coef_r.at[i], dev(1 - s, to, t))
    loop(16, lambda i: coef_copy(i).start())

    loop(16, send_rows, EARLY)

    loop(4, lambda j: ex_copy(j).wait(), 1)
    ebs[...] = (epart[c, x] + ex_in[0] + ex_in[1] + ex_in[2]).astype(BF16)

    def eb_copy(k):
        return remote(ebs.at[pl.ds(k * 32, 32)], eb_in.at[pl.ds((2 * k + s) * 32, 32)],
                      eb_s.at[k], eb_r.at[2 * k + s], dev(1, dest(k), t))

    def send_eb(k):
        @pl.when(is_self(k))
        def _():
            pltpu.make_async_copy(ebs.at[pl.ds(k * 32, 32)], eb_in.at[pl.ds((2 * k + s) * 32, 32)],
                                  eb_r.at[2 * k + s]).start()

        @pl.when(jnp.logical_not(is_self(k)))
        def _():
            eb_copy(k).start()
    loop(16, send_eb)

    def coef_arrived(i):
        frm = (d + 16 - i) % 16
        rows = coef_in.at[pl.ds(frm * 64, 64)]
        pltpu.make_async_copy(rows, rows, coef_r.at[i]).wait()
    loop(16, coef_arrived)

    def unpack_in(src, n):
        blocks = src[...].astype(F32)
        other = pltpu.roll(blocks, 64, 1)
        both = jnp.concatenate([blocks.reshape(HALF // n, 1, n, LANES),
                                other.reshape(HALF // n, 1, n, LANES)], axis=1)
        return both.reshape(TOK, LANES).astype(BF16)

    coefs[:, 0:LANES] = unpack_in(coef_in, 64)

    def put(b):
        own = recv_col[pl.ds(b * LANES, LANES), :]
        hot = jnp.concatenate(
            [jnp.where(own == lane + m * LANES, 1.0, 0.0).astype(BF16) for m in range(16)], axis=1)
        x_in[b // 8, pl.ds((b % 8) * LANES, LANES), :] = jnp.dot(
            hot, coefs[:, 0:LANES], preferred_element_type=F32)
    loop(16, put)

    @pl.when(s == 1)
    def _():
        def eb_arrived(i):
            rows = eb_in.at[pl.ds(i * 32, 32)]
            pltpu.make_async_copy(rows, rows, eb_r.at[i]).wait()
        loop(32, eb_arrived)
        coefs[:, 0:LANES] = unpack_in(eb_in, 32)

        def take(b):
            rows = pl.ds((b % 8) * LANES, LANES)
            x_in[b // 8, rows, :] = x_in[b // 8, rows, :] - jnp.dot(
                place_e[pl.ds(b * LANES, LANES), :], coefs[:, 0:LANES], preferred_element_type=F32)
        loop(16, take)

    gathered[x, c] = jnp.where(half_left, x_in[0], pltpu.roll(x_in[1], 64, 1)).astype(BF16)

    def ag_copy(j):
        return remote(gathered.at[x, c], gathered.at[x, c], ag_s.at[j - 1], ag_r.at[j - 1],
                      dev(s, d, (x + j) % 4 * 2 + c))

    def fwd_copy(j):
        frm = (x + 4 - j) % 4
        return remote(gathered.at[frm, c], gathered.at[frm, c], fwd_s.at[j], fwd_r.at[j], partner)

    loop(4, lambda j: ag_copy(j).start(), 1)
    fwd_copy(0).start()

    def group(g, rows):
        return jnp.dot(place_e[rows, pl.ds(pl.multiple_of(g * 256, 256), 256)],
                       arrived[pl.ds(g * 256, 256), :], preferred_element_type=F32)

    def wait_group(g):
        def one(i):
            rows = arrived.at[pl.ds(i * 64, 64)]
            pltpu.make_async_copy(rows, rows, emb_r.at[i]).wait()
        loop(g * 4 + 4, one, g * 4)

    @pl.when(s == 1)
    def _():
        wait_group(0)

        def first(i):
            rows = pl.ds(i * 256, 256)
            total[rows, :] = group(0, rows)
        loop(8, first)

    @pl.when(s == 0)
    def _():
        def clear(i):
            total[pl.ds(i * 256, 256), :] = jnp.zeros((256, FEAT), F32)
        loop(8, clear)

    def forward(j):
        frm = (x + 4 - j) % 4
        pltpu.make_async_copy(gathered.at[frm, c], gathered.at[frm, c], ag_r.at[j - 1]).wait()
        fwd_copy(j).start()
    loop(4, forward, 1)

    def one_group(g):
        wait_group(g)

        def add(i):
            rows = pl.ds(i * 256, 256)
            total[rows, :] = total[rows, :] + group(g, rows)
        loop(8, add)

    @pl.when(s == 1)
    def _():
        loop(6, one_group, 1)

    def from_partner(j):
        frm = (x + 4 - j) % 4
        pltpu.make_async_copy(gathered.at[frm, 1 - c], gathered.at[frm, 1 - c], fwd_r.at[j]).wait()
    loop(4, from_partner)
    for g in range(4):
        a, b = gathered[g, 0].astype(F32), gathered[g, 1].astype(F32)
        cols = slice(g * LANES, (g + 1) * LANES)
        coefs[0:HALF, cols] = jnp.where(half_left, a, pltpu.roll(b, 64, 1)).astype(BF16)
        coefs[HALF:TOK, cols] = jnp.where(half_left, pltpu.roll(a, 64, 1), b).astype(BF16)

    def lift(i):
        rows = pl.ds(i * 256, 256)
        total[rows, :] = total[rows, :] + lax.dot_general(
            coefs[rows, :], basis[...], (((1,), (1,)), ((), ())), preferred_element_type=F32)
    loop(8, lift)

    @pl.when(s == 1)
    def _():
        loop(8, one_group, 6)

    def out_copy(i):
        rows = pl.ds(i * 256, 256)
        return pltpu.make_async_copy(acts.at[rows], out_hbm.at[rows], out_s.at[i])

    def finish(i):
        rows = pl.ds(i * 256, 256)
        acts[rows, :] = total[rows, :].astype(BF16)
        out_copy(i).start()
    loop(8, finish)

    @pl.when(s == 1)
    def _():
        def asked(i):
            k, so = i // 2, i % 2

            @pl.when((so != 1) | (source(k) != d))
            def _():
                remote(ask.at[0], ask_in.at[0], ask_s.at[i], ask_r.at[0], partner).wait_send()
        loop(32, asked)

    def sent(k):
        coef_copy(k).wait_send()

        @pl.when(jnp.logical_not(is_self(k)))
        def _():
            emb_copy(k).wait_send()
            eb_copy(k).wait_send()
    loop(16, sent)
    loop(4, lambda j: ag_copy(j).wait_send(), 1)
    loop(4, lambda j: fwd_copy(j).wait_send())
    loop(8, lambda i: out_copy(i).wait())


def on_device(outgoing, embedding, shared_basis, token_ids, row_route):
    any_ = pl.BlockSpec(memory_space=pl.ANY)
    vmem = pl.BlockSpec(memory_space=pltpu.VMEM)
    V, D = pltpu.VMEM, pltpu.SemaphoreType.DMA
    scratch = [
        V((TOK, FEAT), BF16), V((VBLOCK, FEAT), BF16), V((LANES, FEAT), BF16), V((FEAT, RANK), BF16),
        V((HALF, FEAT), BF16), V((TOK, FEAT), BF16), V((TOK, FEAT), F32), V((TOK, TOK), BF16),
        V((16, LANES), I32), V((TOK, LANES), I32), V((TOK, LANES), I32), V((TOK, LANES), I32),
        V((16, LANES), I32), V((16, 8, LANES), I32), V((16, 8, LANES), I32), V((LANES, LANES), I32),
        V((2, 4, HALF, LANES), F32), V((4, HALF, LANES), F32), V((3, HALF, LANES), F32),
        V((2, 4, 512, LANES), F32), V((4, 512, LANES), F32), V((3, 512, LANES), F32),
        V((HALF, LANES), BF16), V((HALF, LANES), BF16), V((512, LANES), BF16), V((HALF, LANES), BF16),
        V((4, 2, HALF, LANES), BF16), V((TOK, RANK), BF16),
        D((3,)), D((32,)), D((16,)), D((16,)), D((32,)), D, D, D((3,)), D((3,)),
        D, D, D((3,)), D((3,)), D((16,)), D((16,)), D((16,)), D((32,)),
        D((3,)), D((3,)), D((4,)), D((4,)), D((8,)),
    ]
    out = pl.pallas_call(
        kernel,
        out_shape=jax.ShapeDtypeStruct((TOK, FEAT), BF16),
        in_specs=[any_, any_, any_, vmem, vmem],
        out_specs=any_,
        scratch_shapes=scratch,
        compiler_params=pltpu.CompilerParams(
            collective_id=0, has_side_effects=True, vmem_limit_bytes=62 * 1024 * 1024),
    )(outgoing[0], embedding, shared_basis,
      token_ids.reshape(16, LANES), row_route.reshape(16, LANES))
    return out[None]


def solution(mesh):
    return jax.shard_map(
        on_device,
        mesh=mesh,
        in_specs=(
            P("section", "dp", "tensor"),
            P(("section", "dp"), "tensor"),
            P("tensor", None),
            P("section", "dp"),
            P("section", "dp"),
        ),
        out_specs=P("section", "dp", "tensor"),
        check_vma=False,
    )
```

```python
import jax
import jax.numpy as jnp
from jax import lax
from jax.experimental import pallas as pl
from jax.experimental.pallas import tpu as pltpu
from jax.sharding import PartitionSpec as P

BF16, F32, I32 = jnp.bfloat16, jnp.float32, jnp.int32
TOK = 2048
FEAT = 1024
RANK = 512
VBLOCK = 2008
LANES = 128
HALF = 1024
VWHOLE = 1920
EARLY = 8
NEXT = 12
VIA = (10, 12)


def kernel(acts_hbm, emb_hbm, basis_hbm, ids_ref, route_ref, out_hbm,
           acts, emb, emb_tail, basis, looked, arrived, total, place_e,
           keys, key_col, rank_col, recv_col, send_col, send_row, ask, ask_in, ask_col, relay,
           part, core_in, x_in, epart, ecore_in, ex_out, ex_in,
           slots, coef_in, ebs, eb_in, gathered, coefs,
           load_sem, ask_s, ask_r, emb_s, emb_r, via_r, via_s, core_s, core_r, x_s, x_r,
           ecore_s, ecore_r, ex_s, ex_r, coef_s, coef_r, eb_s, eb_r,
           ag_s, ag_r, fwd_s, fwd_r, out_s):
    s = lax.axis_index("section")
    d = lax.axis_index("dp")
    t = lax.axis_index("tensor")
    y, zh, x, c = d // 4, d % 4, t // 2, t % 2

    def dev(s_, d_, t_):
        return {"section": s_, "dp": d_, "tensor": t_}

    def remote(src, dst, send_sem, recv_sem, to):
        return pltpu.make_async_remote_copy(
            src, dst, send_sem, recv_sem, device_id=to, device_id_type=pl.DeviceIdType.MESH)

    partner = dev(s, d, x * 2 + 1 - c)

    def dy(k):
        return (k // 2) % 4 + 2

    def dz(k):
        return jnp.where(k < 8, 1 + 2 * (k % 2), 2 - 2 * (k % 2))

    def dest(k):
        return (y + dy(k)) % 4 * 4 + (zh + dz(k)) % 4

    def source(k):
        return (y + 8 - dy(k)) % 4 * 4 + (zh + 4 - dz(k)) % 4

    def loop(n, body, start=0):
        def step(i, carry):
            body(i)
            return carry
        lax.fori_loop(start, n, step, 0)

    lane = lax.broadcasted_iota(I32, (LANES, LANES), 1)
    sub = lax.broadcasted_iota(I32, (LANES, LANES), 0)

    load_basis = pltpu.make_async_copy(basis_hbm, basis, load_sem.at[0])
    load_acts = pltpu.make_async_copy(acts_hbm, acts, load_sem.at[1])
    load_emb = pltpu.make_async_copy(emb_hbm, emb, load_sem.at[2])
    load_basis.start()
    load_acts.start()
    load_emb.start()

    barrier = pltpu.get_barrier_semaphore()

    def greet(to):
        pl.semaphore_signal(barrier, inc=1, device_id=to, device_id_type=pl.DeviceIdType.MESH)

    greet(partner)
    loop(4, lambda j: greet(dev(s, d, (x + j) % 4 * 2 + c)), 1)
    loop(16, lambda i: greet(dev(1 - s, (d + i) % 16, t)))

    @pl.when(s == 1)
    def _():
        loop(16, lambda i: greet(dev(s, (d + i) % 16, t)), 1)

    def column(row):
        return jnp.transpose(jnp.broadcast_to(row, (LANES, LANES)))

    def rank_of_columns(dst):
        def block(b):
            own = column(keys[pl.ds(b, 1), :])
            count = jnp.zeros((LANES, LANES), F32)
            for m in range(16):
                count += jnp.where(keys[m:m + 1, :] < own, 1.0, 0.0)
            rank = jnp.sum(count, axis=1, keepdims=True).astype(I32)
            dst[pl.ds(b * LANES, LANES), :] = jnp.broadcast_to(rank, (LANES, LANES))
        loop(16, block)

    pos16 = (lax.broadcasted_iota(I32, (16, LANES), 0) * LANES
             + lax.broadcasted_iota(I32, (16, LANES), 1))

    @pl.when(s == 1)
    def _():
        keys[...] = ids_ref[...] * TOK + pos16
        rank_of_columns(rank_col)

        def id_column(b):
            key_col[pl.ds(b * LANES, LANES), :] = column(ids_ref[pl.ds(b, 1), :])
        loop(16, id_column)

        def request(m):
            found = jnp.zeros((LANES, LANES), I32)
            for b in range(16):
                rows = slice(b * LANES, (b + 1) * LANES)
                found += jnp.where(rank_col[rows, :] == lane + m * LANES, key_col[rows, :], 0)
            ids = jnp.sum(found.astype(F32), axis=0, keepdims=True).astype(I32)
            ask[m] = jnp.broadcast_to(ids, (8, LANES))
        loop(16, request)

    pl.semaphore_wait(barrier, 4 + 16 + 15 * s)

    def ask_owner(i):
        k, so = i // 2, i % 2
        od = source(k)
        src, dst = ask.at[so * 8 + od // 2], ask_in.at[k]

        @pl.when((so == 1) & (od == d))
        def _():
            pltpu.make_async_copy(src, dst, ask_r.at[k]).start()

        @pl.when((so != 1) | (od != d))
        def _():
            remote(src, dst, ask_s.at[i], ask_r.at[k], dev(so, od, t)).start()

    @pl.when(s == 1)
    def _():
        loop(32, ask_owner)

    load_basis.wait()
    load_acts.wait()

    def pack(top, bottom, dst, rows):
        n = top.shape[0]
        left = lax.broadcasted_iota(I32, (n, LANES), 1) < 64
        for g in range(4):
            cols = slice(g * LANES, (g + 1) * LANES)
            a, b = top[:, cols], bottom[:, cols]
            dst[0, g, rows, :] = jnp.where(left, a, pltpu.roll(b, 64, 1))
            dst[1, g, rows, :] = jnp.where(left, pltpu.roll(a, 64, 1), b)

    def project(i):
        top = jnp.dot(acts[pl.ds(i * 256, 256), :], basis[...], preferred_element_type=F32)
        bottom = jnp.dot(acts[pl.ds(HALF + i * 256, 256), :], basis[...], preferred_element_type=F32)
        pack(top, bottom, part, pl.ds(i * 256, 256))
    loop(4, project)

    core_copy = remote(part.at[1 - c], core_in, core_s, core_r, partner)
    core_copy.start()

    load_emb.wait()
    emb_tail[...] = jnp.zeros_like(emb_tail)
    emb_tail[0:VBLOCK - VWHOLE, :] = emb[VWHOLE:VBLOCK, :]
    first_id = (s * 16 + d) * VBLOCK

    def emb_copy(k):
        return remote(looked.at[pl.ds(k * 64, 64)], arrived.at[pl.ds((2 * k + s) * 64, 64)],
                      emb_s.at[k], emb_r.at[2 * k + s], dev(1, dest(k), t))

    def is_self(k):
        return (s == 1) & (dest(k) == d)

    def is_via(k):
        return (s == 1) & ((k == VIA[0]) | (k == VIA[1]))

    def send_rows(k):
        @pl.when(is_self(k))
        def _():
            pltpu.make_async_copy(looked.at[pl.ds(k * 64, 64)], arrived.at[pl.ds((2 * k + s) * 64, 64)],
                                  emb_r.at[2 * k + s]).start()

        @pl.when(jnp.logical_not(is_self(k) | is_via(k)))
        def _():
            emb_copy(k).start()

    def via_copy(i):
        k = VIA[i]
        return remote(looked.at[pl.ds(k * 64, 64)], relay.at[i], emb_s.at[k], via_r.at[i],
                      dev(1, y * 4 + (zh + 1) % 4, t))

    def hand_on(i):
        k = VIA[i]
        return remote(relay.at[i], arrived.at[pl.ds((2 * k + 1) * 64, 64)], via_s.at[i],
                      emb_r.at[2 * k + 1], dev(1, (y + (k // 2) % 4 + 2) % 4 * 4 + (zh + 1) % 4, t))

    def look_up(i):
        for q in range(2):
            k = 2 * i + q
            pltpu.make_async_copy(ask_in.at[k], ask_in.at[k], ask_r.at[k]).wait()
            ask_col[...] = column(ask_in[k, 0:1, :])
            key_col[q * 64:(q + 1) * 64, :] = ask_col[pl.ds((d % 2) * 64, 64), :] - first_id
        want = key_col[0:LANES, :]
        hot = jnp.concatenate(
            [jnp.where(want == lane + m * LANES, 1.0, 0.0).astype(BF16) for m in range(16)], axis=1)
        rows = jnp.dot(hot[:, :VWHOLE], emb[0:VWHOLE, :], preferred_element_type=F32)
        rows += jnp.dot(hot[:, VWHOLE:], emb_tail[...], preferred_element_type=F32)
        looked[pl.ds(i * LANES, LANES), :] = rows.astype(BF16)

    def serve(i):
        look_up(i)
        send_rows(2 * i)
        send_rows(2 * i + 1)
    loop(2, serve)

    core_copy.wait()

    def x_copy(j):
        to = (x + j) % 4
        return remote(part.at[c, to], x_in.at[j - 1], x_s.at[j - 1], x_r.at[j - 1], dev(s, d, to * 2 + c))

    def add_core(j):
        to = (x + j) % 4
        part[c, to] = part[c, to] + core_in[to]

        @pl.when(j < 4)
        def _():
            x_copy(j).start()
    loop(5, add_core, 1)

    loop(EARLY // 2, serve, 2)
    loop(8, look_up, EARLY // 2)

    @pl.when(s == 1)
    def _():
        via_copy(0).start()
        via_copy(1).start()

    def project_rows(i):
        h = jnp.dot(looked[pl.ds(i * 256, 256), :], basis[...], preferred_element_type=F32)
        h = h.reshape(4, 2, 32, RANK)
        pack(h[:, 0].reshape(LANES, RANK), h[:, 1].reshape(LANES, RANK), epart, pl.ds(i * LANES, LANES))
    loop(4, project_rows)
    ecore_copy = remote(epart.at[1 - c], ecore_in, ecore_s, ecore_r, partner)
    ecore_copy.start()

    keys[...] = route_ref[...] - route_ref[...] % TOK + pos16

    def send_column(b):
        key_col[pl.ds(b * LANES, LANES), :] = column(keys[pl.ds(b, 1), :])
    loop(16, send_column)

    def code_of(p):
        return ((p >> 6) & 1) * HALF + (p >> 7) * 64 + (p & 63)

    def send_rank(m):
        own = keys[pl.ds(m, 1), :]
        count = jnp.zeros((LANES, LANES), F32)
        for b in range(16):
            count += jnp.where(key_col[b * LANES:(b + 1) * LANES, :] < own, 1.0, 0.0)
        send_row[pl.ds(m, 1), :] = code_of(jnp.sum(count, axis=0, keepdims=True).astype(I32))
    loop(16, send_rank)

    def invert(b):
        found = jnp.zeros((LANES, LANES), I32)
        for m in range(16):
            found += jnp.where(send_row[m:m + 1, :] == sub + b * LANES, lane + m * LANES, 0)
        row = jnp.sum(found.astype(F32), axis=1, keepdims=True).astype(I32)
        send_col[pl.ds(b * LANES, LANES), :] = jnp.broadcast_to(row, (LANES, LANES))
    loop(16, invert)

    ecore_copy.wait()

    def ex_copy(j):
        to = (x + j) % 4
        return remote(ex_out.at[j - 1], ex_in.at[j - 1], ex_s.at[j - 1], ex_r.at[j - 1], dev(s, d, to * 2 + c))

    def add_ecore(j):
        to = (x + j) % 4
        ex_out[j - 1] = (epart[c, to] + ecore_in[to]).astype(BF16)
        ex_copy(j).start()
    loop(4, add_ecore, 1)

    keys[...] = route_ref[...]
    rank_of_columns(recv_col)

    def recv_code(b):
        rows = pl.ds(b * LANES, LANES)
        recv_col[rows, :] = code_of(recv_col[rows, :])
    loop(16, recv_code)

    @pl.when(s == 1)
    def _():
        def place(b):
            p = rank_col[pl.ds(b * LANES, LANES), :]
            o = p >> 6
            far = (zh + 4 - (o & 3)) & 3
            late = 1 - (far & 1)
            k = late * 8 + ((y + 2 - ((o >> 2) & 3)) & 3) * 2 + ((far >> 1) ^ late)
            code = (2 * k + (o >> 4)) * 64 + (p & 63)
            rank_col[pl.ds(b * LANES, LANES), :] = (
                ((code >> 5) & 1) * HALF + (code >> 6) * 32 + (code & 31))
            for m in range(16):
                place_e[pl.ds(b * LANES, LANES), m * LANES:(m + 1) * LANES] = (
                    jnp.where(code == lane + m * LANES, 1.0, 0.0).astype(BF16))
        loop(16, place)

    loop(4, lambda j: x_copy(j).wait(), 1)
    mine = (part[c, x] + x_in[0] + x_in[1] + x_in[2]).astype(BF16)
    gathered[x, c] = mine
    left = lax.broadcasted_iota(I32, (256, LANES), 1) < 64
    lanes256 = lax.broadcasted_iota(I32, (512, LANES), 1)

    def pick(src, places, use):
        for g in range(4):
            coefs[0:256, g * LANES:(g + 1) * LANES] = src[g * 256:(g + 1) * 256, :]

        def block(i):
            v = jnp.concatenate([places[pl.ds(i * 256, 256), :], places[pl.ds(HALF + i * 256, 256), :]], axis=0)
            low = v & 255
            hot = jnp.concatenate([jnp.where(low == lanes256 + m * LANES, 1.0, 0.0).astype(BF16)
                                   for m in range(2)], axis=1)
            rows = jnp.dot(hot, coefs[0:256, :], preferred_element_type=F32)
            which = (v >> 8) & 3
            found = rows[:, 0:LANES]
            for g in range(1, 4):
                found = jnp.where(which == g, rows[:, g * LANES:(g + 1) * LANES], found)
            other = pltpu.roll(found, 64, 1)
            second = v >= HALF
            top = jnp.where(second[0:256], other[0:256], found[0:256])
            bottom = jnp.where(second[256:512], found[256:512], other[256:512])
            use(pl.ds(i * 256, 256), jnp.where(left, top, bottom))
        loop(4, block)

    def to_slots(rows, value):
        slots[rows, :] = value.astype(BF16)
    pick(gathered.at[x, c], send_col, to_slots)

    def coef_copy(i):
        to = (d + i) % 16
        return remote(slots.at[pl.ds(to * 64, 64)], coef_in.at[pl.ds(d * 64, 64)],
                      coef_s.at[i], coef_r.at[i], dev(1 - s, to, t))
    loop(16, lambda i: coef_copy(i).start())


    @pl.when(s == 1)
    def _():
        for i in range(2):
            pltpu.make_async_copy(relay.at[i], relay.at[i], via_r.at[i]).wait()
            hand_on(i).start()

    loop(NEXT, send_rows, EARLY)

    loop(4, lambda j: ex_copy(j).wait(), 1)
    ebs[...] = (epart[c, x] + ecore_in[x] + ex_in[0].astype(F32) + ex_in[1].astype(F32)
                + ex_in[2].astype(F32)).astype(BF16)

    def eb_copy(k):
        return remote(ebs.at[pl.ds(k * 32, 32)], eb_in.at[pl.ds((2 * k + s) * 32, 32)],
                      eb_s.at[k], eb_r.at[2 * k + s], dev(1, dest(k), t))

    def send_eb(k):
        @pl.when(is_self(k))
        def _():
            pltpu.make_async_copy(ebs.at[pl.ds(k * 32, 32)], eb_in.at[pl.ds((2 * k + s) * 32, 32)],
                                  eb_r.at[2 * k + s]).start()

        @pl.when(jnp.logical_not(is_self(k)))
        def _():
            eb_copy(k).start()
    loop(16, send_eb)

    loop(16, send_rows, NEXT)

    def group(g, rows):
        return jnp.dot(place_e[rows, pl.ds(pl.multiple_of(g * 512, 512), 512)],
                       arrived[pl.ds(g * 512, 512), :], preferred_element_type=F32)

    def wait_group(g):
        def one(i):
            rows = arrived.at[pl.ds(i * 64, 64)]
            pltpu.make_async_copy(rows, rows, emb_r.at[i]).wait()
        loop(g * 8 + 8, one, g * 8)

    def one_group(g):
        wait_group(g)

        def add(i):
            rows = pl.ds(i * 512, 512)
            total[rows, :] = total[rows, :] + group(g, rows)
        loop(4, add)

    @pl.when(s == 1)
    def _():
        wait_group(0)

        def first(i):
            rows = pl.ds(i * 512, 512)
            total[rows, :] = group(0, rows)
        loop(4, first)
        one_group(1)

    def coef_arrived(i):
        frm = (d + 16 - i) % 16
        rows = coef_in.at[pl.ds(frm * 64, 64)]
        pltpu.make_async_copy(rows, rows, coef_r.at[i]).wait()
    loop(16, coef_arrived)

    def put(rows, value):
        x_in[0, rows, :] = value
    pick(coef_in, recv_col, put)

    @pl.when(s == 1)
    def _():
        def eb_arrived(i):
            rows = eb_in.at[pl.ds(i * 32, 32)]
            pltpu.make_async_copy(rows, rows, eb_r.at[i]).wait()
        loop(32, eb_arrived)

        def take(rows, value):
            x_in[0, rows, :] = x_in[0, rows, :] - value
        pick(eb_in, rank_col, take)

    gathered[x, c] = x_in[0].astype(BF16)
    half_left = lax.broadcasted_iota(I32, (HALF, LANES), 1) < 64

    def ag_copy(j):
        return remote(gathered.at[x, c], gathered.at[x, c], ag_s.at[j - 1], ag_r.at[j - 1],
                      dev(s, d, (x + j) % 4 * 2 + c))

    def fwd_copy(j):
        frm = (x + 4 - j) % 4
        return remote(gathered.at[frm, c], gathered.at[frm, c], fwd_s.at[j], fwd_r.at[j], partner)

    loop(4, lambda j: ag_copy(j).start(), 1)
    fwd_copy(0).start()

    def forward(j):
        frm = (x + 4 - j) % 4
        pltpu.make_async_copy(gathered.at[frm, c], gathered.at[frm, c], ag_r.at[j - 1]).wait()
        fwd_copy(j).start()
    loop(4, forward, 1)

    @pl.when(s == 1)
    def _():
        one_group(2)

    def from_partner(j):
        frm = (x + 4 - j) % 4
        pltpu.make_async_copy(gathered.at[frm, 1 - c], gathered.at[frm, 1 - c], fwd_r.at[j]).wait()
    loop(4, from_partner)
    for g in range(4):
        a, b = gathered[g, 0].astype(F32), gathered[g, 1].astype(F32)
        cols = slice(g * LANES, (g + 1) * LANES)
        coefs[0:HALF, cols] = jnp.where(half_left, a, pltpu.roll(b, 64, 1)).astype(BF16)
        coefs[HALF:TOK, cols] = jnp.where(half_left, pltpu.roll(a, 64, 1), b).astype(BF16)

    def lifted(rows):
        return lax.dot_general(
            coefs[rows, :], basis[...], (((1,), (1,)), ((), ())), preferred_element_type=F32)

    def out_copy(i):
        rows = pl.ds(i * 512, 512)
        return pltpu.make_async_copy(acts.at[rows], out_hbm.at[rows], out_s.at[i])

    @pl.when(s == 0)
    def _():
        def finish(i):
            rows = pl.ds(i * 512, 512)
            acts[rows, :] = lifted(rows).astype(BF16)
            out_copy(i).start()
        loop(4, finish)

    @pl.when(s == 1)
    def _():
        def lift(i):
            rows = pl.ds(i * 512, 512)
            total[rows, :] = total[rows, :] + lifted(rows)
        loop(4, lift)
        wait_group(3)

        def finish(i):
            rows = pl.ds(i * 512, 512)
            acts[rows, :] = (total[rows, :] + group(3, rows)).astype(BF16)
            out_copy(i).start()
        loop(4, finish)

    @pl.when(s == 1)
    def _():
        def asked(i):
            k, so = i // 2, i % 2

            @pl.when((so != 1) | (source(k) != d))
            def _():
                remote(ask.at[0], ask_in.at[0], ask_s.at[i], ask_r.at[0], partner).wait_send()
        loop(32, asked)

    def sent(k):
        coef_copy(k).wait_send()

        @pl.when(jnp.logical_not(is_self(k)))
        def _():
            emb_copy(k).wait_send()
            eb_copy(k).wait_send()
    loop(16, sent)

    @pl.when(s == 1)
    def _():
        hand_on(0).wait_send()
        hand_on(1).wait_send()
    loop(4, lambda j: ag_copy(j).wait_send(), 1)
    loop(4, lambda j: fwd_copy(j).wait_send())
    loop(4, lambda i: out_copy(i).wait())


def on_device(outgoing, embedding, shared_basis, token_ids, row_route):
    any_ = pl.BlockSpec(memory_space=pl.ANY)
    vmem = pl.BlockSpec(memory_space=pltpu.VMEM)
    V, D = pltpu.VMEM, pltpu.SemaphoreType.DMA
    scratch = [
        V((TOK, FEAT), BF16), V((VBLOCK, FEAT), BF16), V((LANES, FEAT), BF16), V((FEAT, RANK), BF16),
        V((HALF, FEAT), BF16), V((TOK, FEAT), BF16), V((TOK, FEAT), F32), V((TOK, TOK), BF16),
        V((16, LANES), I32), V((TOK, LANES), I32), V((TOK, LANES), I32), V((TOK, LANES), I32), V((TOK, LANES), I32),
        V((16, LANES), I32), V((16, 8, LANES), I32), V((16, 8, LANES), I32), V((LANES, LANES), I32),
        V((2, 64, FEAT), BF16),
        V((2, 4, HALF, LANES), F32), V((4, HALF, LANES), F32), V((3, HALF, LANES), F32),
        V((2, 4, 512, LANES), F32), V((4, 512, LANES), F32), V((3, 512, LANES), BF16), V((3, 512, LANES), BF16),
        V((HALF, LANES), BF16), V((HALF, LANES), BF16), V((512, LANES), BF16), V((HALF, LANES), BF16),
        V((4, 2, HALF, LANES), BF16), V((TOK, RANK), BF16),
        D((3,)), D((32,)), D((16,)), D((16,)), D((32,)), D((2,)), D((2,)), D, D, D((3,)), D((3,)),
        D, D, D((3,)), D((3,)), D((16,)), D((16,)), D((16,)), D((32,)),
        D((3,)), D((3,)), D((4,)), D((4,)), D((4,)),
    ]
    out = pl.pallas_call(
        kernel,
        out_shape=jax.ShapeDtypeStruct((TOK, FEAT), BF16),
        in_specs=[any_, any_, any_, vmem, vmem],
        out_specs=any_,
        scratch_shapes=scratch,
        compiler_params=pltpu.CompilerParams(
            collective_id=0, has_side_effects=True, vmem_limit_bytes=62 * 1024 * 1024),
    )(outgoing[0], embedding, shared_basis,
      token_ids.reshape(16, LANES), row_route.reshape(16, LANES))
    return out[None]


def solution(mesh):
    return jax.shard_map(
        on_device,
        mesh=mesh,
        in_specs=(
            P("section", "dp", "tensor"),
            P(("section", "dp"), "tensor"),
            P("tensor", None),
            P("section", "dp"),
            P("section", "dp"),
        ),
        out_specs=P("section", "dp", "tensor"),
        check_vma=False,
    )
```

```python
import jax
import jax.numpy as jnp
from jax import lax
from jax.experimental import pallas as pl
from jax.experimental.pallas import tpu as pltpu
from jax.sharding import PartitionSpec as P

BF16, F32, I32 = jnp.bfloat16, jnp.float32, jnp.int32
TOK = 2048
FEAT = 1024
RANK = 512
VBLOCK = 2008
LANES = 128
HALF = 1024
VWHOLE = 1920
EARLY = 10
NEXT = 10
VIA = (0, 2)


def kernel(acts_hbm, emb_hbm, basis_hbm, ids_ref, route_ref, acts, emb, emb_tail, basis, looked, arrived, total, place_e,
           keys, key_col, rank_col, recv_col, send_col, send_row, ask, ask_in, ask_col, relay,
           part, core_in, x_in, epart, ecore_in, ex_out, ex_in,
           slots, coef_in, ebs, eb_in, gathered, coefs,
           load_sem, ask_s, ask_r, emb_s, emb_r, via_r, via_s, core_s, core_r, x_s, x_r,
           ecore_s, ecore_r, ex_s, ex_r, coef_s, coef_r, eb_s, eb_r,
           ag_s, ag_r, fwd_s, fwd_r):
    s = lax.axis_index("section")
    d = lax.axis_index("dp")
    t = lax.axis_index("tensor")
    y, zh, x, c = d // 4, d % 4, t // 2, t % 2

    def dev(s_, d_, t_):
        return {"section": s_, "dp": d_, "tensor": t_}

    def remote(src, dst, send_sem, recv_sem, to):
        return pltpu.make_async_remote_copy(
            src, dst, send_sem, recv_sem, device_id=to, device_id_type=pl.DeviceIdType.MESH)

    partner = dev(s, d, x * 2 + 1 - c)

    def near(k):
        return (k >= 4) & (k < 12)

    def dy(k):
        return jnp.where(near(k), (k + 12) // 2, jnp.where(k < 4, k + 6, k + 14) // 2) % 4

    def dz(k):
        return jnp.where(near(k), 1 + 2 * (k % 2), 2 - 2 * (k % 2))

    def dest(k):
        return (y + dy(k)) % 4 * 4 + (zh + dz(k)) % 4

    def source(k):
        return (y + 4 - dy(k)) % 4 * 4 + (zh + 4 - dz(k)) % 4

    def loop(n, body, start=0):
        def step(i, carry):
            body(i)
            return carry
        lax.fori_loop(start, n, step, 0)

    lane = lax.broadcasted_iota(I32, (LANES, LANES), 1)
    sub = lax.broadcasted_iota(I32, (LANES, LANES), 0)

    load_basis = pltpu.make_async_copy(basis_hbm, basis, load_sem.at[0])
    load_acts = pltpu.make_async_copy(acts_hbm, acts, load_sem.at[1])
    load_emb = pltpu.make_async_copy(emb_hbm, emb, load_sem.at[2])
    load_basis.start()
    load_acts.start()
    load_emb.start()

    barrier = pltpu.get_barrier_semaphore()

    def greet(to):
        pl.semaphore_signal(barrier, inc=1, device_id=to, device_id_type=pl.DeviceIdType.MESH)

    greet(partner)
    loop(4, lambda j: greet(dev(s, d, (x + j) % 4 * 2 + c)), 1)
    loop(16, lambda i: greet(dev(1 - s, (d + i) % 16, t)))

    @pl.when(s == 1)
    def _():
        loop(16, lambda i: greet(dev(s, (d + i) % 16, t)), 1)

    def column(row):
        return jnp.transpose(jnp.broadcast_to(row, (LANES, LANES)))

    def rank_of_columns(dst):
        def block(b):
            own = column(keys[pl.ds(b, 1), :])
            count = jnp.zeros((LANES, LANES), F32)
            for m in range(16):
                count += jnp.where(keys[m:m + 1, :] < own, 1.0, 0.0)
            rank = jnp.sum(count, axis=1, keepdims=True).astype(I32)
            dst[pl.ds(b * LANES, LANES), :] = jnp.broadcast_to(rank, (LANES, LANES))
        loop(16, block)

    pos16 = (lax.broadcasted_iota(I32, (16, LANES), 0) * LANES
             + lax.broadcasted_iota(I32, (16, LANES), 1))

    @pl.when(s == 1)
    def _():
        keys[...] = ids_ref[...] * TOK + pos16
        rank_of_columns(rank_col)

        def id_column(b):
            key_col[pl.ds(b * LANES, LANES), :] = column(ids_ref[pl.ds(b, 1), :])
        loop(16, id_column)

        def request(m):
            found = jnp.zeros((LANES, LANES), I32)
            for b in range(16):
                rows = slice(b * LANES, (b + 1) * LANES)
                found += jnp.where(rank_col[rows, :] == lane + m * LANES, key_col[rows, :], 0)
            ids = jnp.sum(found.astype(F32), axis=0, keepdims=True).astype(I32)
            ask[m] = jnp.broadcast_to(ids, (8, LANES))
        loop(16, request)

    pl.semaphore_wait(barrier, 4 + 16 + 15 * s)

    def ask_owner(i):
        k, so = i // 2, i % 2
        od = source(k)
        src, dst = ask.at[so * 8 + od // 2], ask_in.at[k]

        @pl.when((so == 1) & (od == d))
        def _():
            pltpu.make_async_copy(src, dst, ask_r.at[k]).start()

        @pl.when((so != 1) | (od != d))
        def _():
            remote(src, dst, ask_s.at[i], ask_r.at[k], dev(so, od, t)).start()

    @pl.when(s == 1)
    def _():
        loop(32, ask_owner)

    load_basis.wait()
    load_acts.wait()

    def pack(top, bottom, dst, rows):
        n = top.shape[0]
        left = lax.broadcasted_iota(I32, (n, LANES), 1) < 64
        for g in range(4):
            cols = slice(g * LANES, (g + 1) * LANES)
            a, b = top[:, cols], bottom[:, cols]
            dst[0, g, rows, :] = jnp.where(left, a, pltpu.roll(b, 64, 1))
            dst[1, g, rows, :] = jnp.where(left, pltpu.roll(a, 64, 1), b)

    def project(i):
        top = jnp.dot(acts[pl.ds(i * 256, 256), :], basis[...], preferred_element_type=F32)
        bottom = jnp.dot(acts[pl.ds(HALF + i * 256, 256), :], basis[...], preferred_element_type=F32)
        pack(top, bottom, part, pl.ds(i * 256, 256))
    loop(4, project)

    core_copy = remote(part.at[1 - c], core_in, core_s, core_r, partner)
    core_copy.start()

    load_emb.wait()
    emb_tail[...] = jnp.zeros_like(emb_tail)
    emb_tail[0:VBLOCK - VWHOLE, :] = emb[VWHOLE:VBLOCK, :]
    first_id = (s * 16 + d) * VBLOCK

    def emb_copy(k):
        return remote(looked.at[pl.ds(k * 64, 64)], arrived.at[pl.ds((2 * k + s) * 64, 64)],
                      emb_s.at[k], emb_r.at[2 * k + s], dev(1, dest(k), t))

    def is_self(k):
        return (s == 1) & (dest(k) == d)

    def is_via(k):
        return (s == 1) & ((k == VIA[0]) | (k == VIA[1]))

    def send_rows(k):
        @pl.when(is_self(k))
        def _():
            pltpu.make_async_copy(looked.at[pl.ds(k * 64, 64)], arrived.at[pl.ds((2 * k + s) * 64, 64)],
                                  emb_r.at[2 * k + s]).start()

        @pl.when(jnp.logical_not(is_self(k) | is_via(k)))
        def _():
            emb_copy(k).start()

        @pl.when(is_via(k))
        def _():
            via_copy(k // 2).start()

    def via_copy(i):
        k = 2 * i
        return remote(looked.at[pl.ds(k * 64, 64)], relay.at[i], emb_s.at[k], via_r.at[i],
                      dev(1, y * 4 + (zh + 1) % 4, t))

    def hand_on(i):
        k = VIA[i]
        return remote(relay.at[i], arrived.at[pl.ds((2 * k + 1) * 64, 64)], via_s.at[i],
                      emb_r.at[2 * k + 1], dev(1, (y + dy(k)) % 4 * 4 + (zh + 1) % 4, t))

    def look_up(i):
        for q in range(2):
            k = 2 * i + q
            pltpu.make_async_copy(ask_in.at[k], ask_in.at[k], ask_r.at[k]).wait()
            ask_col[...] = column(ask_in[k, 0:1, :])
            key_col[q * 64:(q + 1) * 64, :] = ask_col[pl.ds((d % 2) * 64, 64), :] - first_id
        want = key_col[0:LANES, :]
        hot = jnp.concatenate(
            [jnp.where(want == lane + m * LANES, 1.0, 0.0).astype(BF16) for m in range(16)], axis=1)
        rows = jnp.dot(hot[:, :VWHOLE], emb[0:VWHOLE, :], preferred_element_type=F32)
        rows += jnp.dot(hot[:, VWHOLE:], emb_tail[...], preferred_element_type=F32)
        looked[pl.ds(i * LANES, LANES), :] = rows.astype(BF16)

    def serve(i):
        look_up(i)
        send_rows(2 * i)
        send_rows(2 * i + 1)
    loop(2, serve)

    core_copy.wait()

    def x_copy(j):
        to = (x + j) % 4
        return remote(part.at[c, to], x_in.at[j - 1], x_s.at[j - 1], x_r.at[j - 1], dev(s, d, to * 2 + c))

    def add_core(j):
        to = (x + j) % 4
        part[c, to] = part[c, to] + core_in[to]

        @pl.when(j < 4)
        def _():
            x_copy(j).start()
    loop(5, add_core, 1)

    loop(EARLY // 2, serve, 2)
    loop(8, look_up, EARLY // 2)

    def project_rows(i):
        h = jnp.dot(looked[pl.ds(i * 256, 256), :], basis[...], preferred_element_type=F32)
        h = h.reshape(4, 2, 32, RANK)
        pack(h[:, 0].reshape(LANES, RANK), h[:, 1].reshape(LANES, RANK), epart, pl.ds(i * LANES, LANES))
    loop(4, project_rows)
    ecore_copy = remote(epart.at[1 - c], ecore_in, ecore_s, ecore_r, partner)
    ecore_copy.start()

    @pl.when(s == 1)
    def _():
        for i in range(2):
            pltpu.make_async_copy(relay.at[i], relay.at[i], via_r.at[i]).wait()
            hand_on(i).start()

    keys[...] = route_ref[...] - route_ref[...] % TOK + pos16

    def send_column(b):
        key_col[pl.ds(b * LANES, LANES), :] = column(keys[pl.ds(b, 1), :])
    loop(16, send_column)

    def code_of(p):
        return ((p >> 6) & 1) * HALF + (p >> 7) * 64 + (p & 63)

    def send_rank(m):
        own = keys[pl.ds(m, 1), :]
        count = jnp.zeros((LANES, LANES), F32)
        for b in range(16):
            count += jnp.where(key_col[b * LANES:(b + 1) * LANES, :] < own, 1.0, 0.0)
        send_row[pl.ds(m, 1), :] = code_of(jnp.sum(count, axis=0, keepdims=True).astype(I32))
    loop(16, send_rank)

    def invert(b):
        found = jnp.zeros((LANES, LANES), I32)
        for m in range(16):
            found += jnp.where(send_row[m:m + 1, :] == sub + b * LANES, lane + m * LANES, 0)
        row = jnp.sum(found.astype(F32), axis=1, keepdims=True).astype(I32)
        send_col[pl.ds(b * LANES, LANES), :] = jnp.broadcast_to(row, (LANES, LANES))
    loop(16, invert)

    ecore_copy.wait()

    def ex_copy(j):
        to = (x + j) % 4
        return remote(ex_out.at[j - 1], ex_in.at[j - 1], ex_s.at[j - 1], ex_r.at[j - 1], dev(s, d, to * 2 + c))

    def add_ecore(j):
        to = (x + j) % 4
        ex_out[j - 1] = (epart[c, to] + ecore_in[to]).astype(BF16)
        ex_copy(j).start()
    loop(4, add_ecore, 1)

    keys[...] = route_ref[...]
    rank_of_columns(recv_col)

    def recv_code(b):
        rows = pl.ds(b * LANES, LANES)
        recv_col[rows, :] = code_of(recv_col[rows, :])
    loop(16, recv_code)

    @pl.when(s == 1)
    def _():
        def place(b):
            p = rank_col[pl.ds(b * LANES, LANES), :]
            o = p >> 6
            to_y, to_z = (y + 4 - ((o >> 2) & 3)) & 3, (zh + 4 - (o & 3)) & 3
            odd = to_z & 1
            e = ((to_y + 1) & 3) * 2 + 1 - (to_z >> 1)
            k = jnp.where(odd == 1, 4 + to_y * 2 + (to_z >> 1), e + 8 * (e >> 2))
            code = (2 * k + (o >> 4)) * 64 + (p & 63)
            rank_col[pl.ds(b * LANES, LANES), :] = (
                ((code >> 5) & 1) * HALF + (code >> 6) * 32 + (code & 31))
            for m in range(16):
                place_e[pl.ds(b * LANES, LANES), m * LANES:(m + 1) * LANES] = (
                    jnp.where(code == lane + m * LANES, 1.0, 0.0).astype(BF16))
        loop(16, place)

    loop(4, lambda j: x_copy(j).wait(), 1)
    mine = (part[c, x] + x_in[0] + x_in[1] + x_in[2]).astype(BF16)
    gathered[x, c] = mine
    left = lax.broadcasted_iota(I32, (256, LANES), 1) < 64
    lanes256 = lax.broadcasted_iota(I32, (512, LANES), 1)

    def pick(src, places, use):
        for g in range(4):
            coefs[0:256, g * LANES:(g + 1) * LANES] = src[g * 256:(g + 1) * 256, :]

        def block(i):
            v = jnp.concatenate([places[pl.ds(i * 256, 256), :], places[pl.ds(HALF + i * 256, 256), :]], axis=0)
            low = v & 255
            hot = jnp.concatenate([jnp.where(low == lanes256 + m * LANES, 1.0, 0.0).astype(BF16)
                                   for m in range(2)], axis=1)
            rows = jnp.dot(hot, coefs[0:256, :], preferred_element_type=F32)
            which = (v >> 8) & 3
            found = rows[:, 0:LANES]
            for g in range(1, 4):
                found = jnp.where(which == g, rows[:, g * LANES:(g + 1) * LANES], found)
            other = pltpu.roll(found, 64, 1)
            second = v >= HALF
            top = jnp.where(second[0:256], other[0:256], found[0:256])
            bottom = jnp.where(second[256:512], found[256:512], other[256:512])
            use(pl.ds(i * 256, 256), jnp.where(left, top, bottom))
        loop(4, block)

    def to_slots(rows, value):
        slots[rows, :] = value.astype(BF16)
    pick(gathered.at[x, c], send_col, to_slots)

    def coef_copy(i):
        to = (d + i) % 16
        return remote(slots.at[pl.ds(to * 64, 64)], coef_in.at[pl.ds(d * 64, 64)],
                      coef_s.at[i], coef_r.at[i], dev(1 - s, to, t))
    loop(16, lambda i: coef_copy(i).start())


    loop(NEXT, send_rows, EARLY)

    loop(4, lambda j: ex_copy(j).wait(), 1)
    ebs[...] = (epart[c, x] + ecore_in[x] + ex_in[0].astype(F32) + ex_in[1].astype(F32)
                + ex_in[2].astype(F32)).astype(BF16)

    def eb_copy(k):
        return remote(ebs.at[pl.ds(k * 32, 32)], eb_in.at[pl.ds((2 * k + s) * 32, 32)],
                      eb_s.at[k], eb_r.at[2 * k + s], dev(1, dest(k), t))

    def send_eb(k):
        @pl.when(is_self(k))
        def _():
            pltpu.make_async_copy(ebs.at[pl.ds(k * 32, 32)], eb_in.at[pl.ds((2 * k + s) * 32, 32)],
                                  eb_r.at[2 * k + s]).start()

        @pl.when(jnp.logical_not(is_self(k)))
        def _():
            eb_copy(k).start()
    loop(16, send_eb)

    loop(16, send_rows, NEXT)

    def group(g, rows):
        return jnp.dot(place_e[rows, pl.ds(pl.multiple_of(g * 512, 512), 512)],
                       arrived[pl.ds(g * 512, 512), :], preferred_element_type=F32)

    def wait_group(g):
        def one(i):
            rows = arrived.at[pl.ds(i * 64, 64)]
            pltpu.make_async_copy(rows, rows, emb_r.at[i]).wait()
        loop(g * 8 + 8, one, g * 8)

    def one_group(g):
        wait_group(g)

        def add(i):
            rows = pl.ds(i * 512, 512)
            total[rows, :] = total[rows, :] + group(g, rows)
        loop(4, add)

    @pl.when(s == 1)
    def _():
        wait_group(0)

        def first(i):
            rows = pl.ds(i * 512, 512)
            total[rows, :] = group(0, rows)
        loop(4, first)
        one_group(1)

    def coef_arrived(i):
        frm = (d + 16 - i) % 16
        rows = coef_in.at[pl.ds(frm * 64, 64)]
        pltpu.make_async_copy(rows, rows, coef_r.at[i]).wait()
    loop(16, coef_arrived)

    def put(rows, value):
        x_in[0, rows, :] = value
    pick(coef_in, recv_col, put)

    @pl.when(s == 1)
    def _():
        def eb_arrived(i):
            rows = eb_in.at[pl.ds(i * 32, 32)]
            pltpu.make_async_copy(rows, rows, eb_r.at[i]).wait()
        loop(32, eb_arrived)

        def take(rows, value):
            x_in[0, rows, :] = x_in[0, rows, :] - value
        pick(eb_in, rank_col, take)

    gathered[x, c] = x_in[0].astype(BF16)
    half_left = lax.broadcasted_iota(I32, (HALF, LANES), 1) < 64

    def ag_copy(j):
        return remote(gathered.at[x, c], gathered.at[x, c], ag_s.at[j - 1], ag_r.at[j - 1],
                      dev(s, d, (x + j) % 4 * 2 + c))

    def fwd_copy(j):
        frm = (x + 4 - j) % 4
        return remote(gathered.at[frm, c], gathered.at[frm, c], fwd_s.at[j], fwd_r.at[j], partner)

    loop(4, lambda j: ag_copy(j).start(), 1)
    fwd_copy(0).start()

    def forward(j):
        frm = (x + 4 - j) % 4
        pltpu.make_async_copy(gathered.at[frm, c], gathered.at[frm, c], ag_r.at[j - 1]).wait()
        fwd_copy(j).start()
    loop(4, forward, 1)

    @pl.when(s == 1)
    def _():
        one_group(2)

    def from_partner(j):
        frm = (x + 4 - j) % 4
        pltpu.make_async_copy(gathered.at[frm, 1 - c], gathered.at[frm, 1 - c], fwd_r.at[j]).wait()
    loop(4, from_partner)
    for g in range(4):
        a, b = gathered[g, 0].astype(F32), gathered[g, 1].astype(F32)
        cols = slice(g * LANES, (g + 1) * LANES)
        coefs[0:HALF, cols] = jnp.where(half_left, a, pltpu.roll(b, 64, 1)).astype(BF16)
        coefs[HALF:TOK, cols] = jnp.where(half_left, pltpu.roll(a, 64, 1), b).astype(BF16)

    def lifted(rows):
        return lax.dot_general(
            coefs[rows, :], basis[...], (((1,), (1,)), ((), ())), preferred_element_type=F32)

    @pl.when(s == 0)
    def _():
        def finish(i):
            rows = pl.ds(i * 512, 512)
            acts[rows, :] = lifted(rows).astype(BF16)
        loop(4, finish)

    @pl.when(s == 1)
    def _():
        def lift(i):
            rows = pl.ds(i * 512, 512)
            total[rows, :] = total[rows, :] + lifted(rows)
        loop(4, lift)
        wait_group(3)

        def finish(i):
            rows = pl.ds(i * 512, 512)
            acts[rows, :] = (total[rows, :] + group(3, rows)).astype(BF16)
        loop(4, finish)

    @pl.when(s == 1)
    def _():
        def asked(i):
            k, so = i // 2, i % 2

            @pl.when((so != 1) | (source(k) != d))
            def _():
                remote(ask.at[0], ask_in.at[0], ask_s.at[i], ask_r.at[0], partner).wait_send()
        loop(32, asked)

    def sent(k):
        coef_copy(k).wait_send()

        @pl.when(jnp.logical_not(is_self(k)))
        def _():
            emb_copy(k).wait_send()
            eb_copy(k).wait_send()
    loop(16, sent)

    @pl.when(s == 1)
    def _():
        hand_on(0).wait_send()
        hand_on(1).wait_send()
    loop(4, lambda j: ag_copy(j).wait_send(), 1)
    loop(4, lambda j: fwd_copy(j).wait_send())


def on_device(outgoing, embedding, shared_basis, token_ids, row_route):
    any_ = pl.BlockSpec(memory_space=pl.ANY)
    vmem = pl.BlockSpec(memory_space=pltpu.VMEM)
    V, D = pltpu.VMEM, pltpu.SemaphoreType.DMA
    scratch = [
        V((VBLOCK, FEAT), BF16), V((LANES, FEAT), BF16), V((FEAT, RANK), BF16),
        V((HALF, FEAT), BF16), V((TOK, FEAT), BF16), V((TOK, FEAT), F32), V((TOK, TOK), BF16),
        V((16, LANES), I32), V((TOK, LANES), I32), V((TOK, LANES), I32), V((TOK, LANES), I32), V((TOK, LANES), I32),
        V((16, LANES), I32), V((16, 8, LANES), I32), V((16, 8, LANES), I32), V((LANES, LANES), I32),
        V((2, 64, FEAT), BF16),
        V((2, 4, HALF, LANES), F32), V((4, HALF, LANES), F32), V((3, HALF, LANES), F32),
        V((2, 4, 512, LANES), F32), V((4, 512, LANES), F32), V((3, 512, LANES), BF16), V((3, 512, LANES), BF16),
        V((HALF, LANES), BF16), V((HALF, LANES), BF16), V((512, LANES), BF16), V((HALF, LANES), BF16),
        V((4, 2, HALF, LANES), BF16), V((TOK, RANK), BF16),
        D((3,)), D((32,)), D((16,)), D((16,)), D((32,)), D((2,)), D((2,)), D, D, D((3,)), D((3,)),
        D, D, D((3,)), D((3,)), D((16,)), D((16,)), D((16,)), D((32,)),
        D((3,)), D((3,)), D((4,)), D((4,)),
    ]
    out = pl.pallas_call(
        kernel,
        out_shape=pltpu.VMEM((TOK, FEAT), BF16),
        in_specs=[any_, any_, any_, vmem, vmem],
        out_specs=vmem,
        scratch_shapes=scratch,
        compiler_params=pltpu.CompilerParams(
            collective_id=0, has_side_effects=True, vmem_limit_bytes=57 * 1024 * 1024),
    )(outgoing[0], embedding, shared_basis,
      token_ids.reshape(16, LANES), row_route.reshape(16, LANES))
    return out[None]


def solution(mesh):
    return jax.shard_map(
        on_device,
        mesh=mesh,
        in_specs=(
            P("section", "dp", "tensor"),
            P(("section", "dp"), "tensor"),
            P("tensor", None),
            P("section", "dp"),
            P("section", "dp"),
        ),
        out_specs=P("section", "dp", "tensor"),
        check_vma=False,
    )
```

```python
import jax
import jax.numpy as jnp
from jax import lax
from jax.experimental import pallas as pl
from jax.experimental.pallas import tpu as pltpu
from jax.sharding import PartitionSpec as P

BF16, F32, I32 = jnp.bfloat16, jnp.float32, jnp.int32
TOK = 2048
FEAT = 1024
RANK = 512
VBLOCK = 2008
LANES = 128
HALF = 1024
VWHOLE = 1920
EARLY = 8
VIA = (0, 2)


def kernel(acts_hbm, emb_hbm, basis_hbm, ids_ref, route_ref, acts, emb, emb_tail, basis, looked, arrived, total, place_e,
           keys, key_col, rank_col, recv_col, send_col, send_row, ask, ask_in, ask_col, relay,
           part, core_in, x_out, x_in, epart, ecore_in, ex_out, ex_in,
           slots, coef_in, ebs, eb_in, gathered, coefs,
           load_sem, ask_s, ask_r, emb_s, emb_r, via_r, via_s, core_s, core_r, x_s, x_r,
           ecore_s, ecore_r, ex_s, ex_r, coef_s, coef_r, eb_s, eb_r,
           ag_s, ag_r, fwd_s, fwd_r):
    s = lax.axis_index("section")
    d = lax.axis_index("dp")
    t = lax.axis_index("tensor")
    y, zh, x, c = d // 4, d % 4, t // 2, t % 2

    def dev(s_, d_, t_):
        return {"section": s_, "dp": d_, "tensor": t_}

    def remote(src, dst, send_sem, recv_sem, to):
        return pltpu.make_async_remote_copy(
            src, dst, send_sem, recv_sem, device_id=to, device_id_type=pl.DeviceIdType.MESH)

    partner = dev(s, d, x * 2 + 1 - c)

    def near(k):
        return (k >= 4) & (k < 12)

    def dy(k):
        return jnp.where(near(k), (k + 12) // 2, jnp.where(k < 4, k + 6, k + 14) // 2) % 4

    def dz(k):
        return jnp.where(near(k), 1 + 2 * (k % 2), 2 - 2 * (k % 2))

    def dest(k):
        return (y + dy(k)) % 4 * 4 + (zh + dz(k)) % 4

    def source(k):
        return (y + 4 - dy(k)) % 4 * 4 + (zh + 4 - dz(k)) % 4

    def loop(n, body, start=0):
        def step(i, carry):
            body(i)
            return carry
        lax.fori_loop(start, n, step, 0)

    lane = lax.broadcasted_iota(I32, (LANES, LANES), 1)
    sub = lax.broadcasted_iota(I32, (LANES, LANES), 0)

    load_basis = pltpu.make_async_copy(basis_hbm, basis, load_sem.at[0])
    load_acts = pltpu.make_async_copy(acts_hbm, acts, load_sem.at[1])
    load_emb = pltpu.make_async_copy(emb_hbm, emb, load_sem.at[2])
    load_basis.start()
    load_acts.start()
    load_emb.start()

    barrier = pltpu.get_barrier_semaphore()

    def greet(to):
        pl.semaphore_signal(barrier, inc=1, device_id=to, device_id_type=pl.DeviceIdType.MESH)

    greet(partner)
    loop(4, lambda j: greet(dev(s, d, (x + j) % 4 * 2 + c)), 1)
    loop(16, lambda i: greet(dev(1 - s, (d + i) % 16, t)))

    @pl.when(s == 1)
    def _():
        loop(16, lambda i: greet(dev(s, (d + i) % 16, t)), 1)

    def column(row):
        return jnp.transpose(jnp.broadcast_to(row, (LANES, LANES)))

    def rank_of_columns(dst):
        def block(b):
            own = column(keys[pl.ds(b, 1), :])
            count = jnp.zeros((LANES, LANES), F32)
            for m in range(16):
                count += jnp.where(keys[m:m + 1, :] < own, 1.0, 0.0)
            rank = jnp.sum(count, axis=1, keepdims=True).astype(I32)
            dst[pl.ds(b * LANES, LANES), :] = jnp.broadcast_to(rank, (LANES, LANES))
        loop(16, block)

    pos16 = (lax.broadcasted_iota(I32, (16, LANES), 0) * LANES
             + lax.broadcasted_iota(I32, (16, LANES), 1))

    @pl.when(s == 1)
    def _():
        keys[...] = ids_ref[...] * TOK + pos16
        rank_of_columns(rank_col)

        def id_column(b):
            key_col[pl.ds(b * LANES, LANES), :] = column(ids_ref[pl.ds(b, 1), :])
        loop(16, id_column)

        def request(m):
            found = jnp.zeros((LANES, LANES), I32)
            for b in range(16):
                rows = slice(b * LANES, (b + 1) * LANES)
                found += jnp.where(rank_col[rows, :] == lane + m * LANES, key_col[rows, :], 0)
            ids = jnp.sum(found.astype(F32), axis=0, keepdims=True).astype(I32)
            ask[m] = jnp.broadcast_to(ids, (8, LANES))
        loop(16, request)

    pl.semaphore_wait(barrier, 4 + 16 + 15 * s)

    def ask_owner(i):
        k, so = i // 2, i % 2
        od = source(k)
        src, dst = ask.at[so * 8 + od // 2], ask_in.at[k]

        @pl.when((so == 1) & (od == d))
        def _():
            pltpu.make_async_copy(src, dst, ask_r.at[k]).start()

        @pl.when((so != 1) | (od != d))
        def _():
            remote(src, dst, ask_s.at[i], ask_r.at[k], dev(so, od, t)).start()

    @pl.when(s == 1)
    def _():
        loop(32, ask_owner)

    load_basis.wait()
    load_acts.wait()

    def pack(top, bottom, dst, rows):
        n = top.shape[0]
        left = lax.broadcasted_iota(I32, (n, LANES), 1) < 64
        for g in range(4):
            cols = slice(g * LANES, (g + 1) * LANES)
            a, b = top[:, cols], bottom[:, cols]
            dst[0, g, rows, :] = jnp.where(left, a, pltpu.roll(b, 64, 1))
            dst[1, g, rows, :] = jnp.where(left, pltpu.roll(a, 64, 1), b)

    def project(i):
        top = jnp.dot(acts[pl.ds(i * 256, 256), :], basis[...], preferred_element_type=F32)
        bottom = jnp.dot(acts[pl.ds(HALF + i * 256, 256), :], basis[...], preferred_element_type=F32)
        pack(top, bottom, part, pl.ds(i * 256, 256))
    loop(4, project)

    core_copy = remote(part.at[1 - c], core_in, core_s, core_r, partner)
    core_copy.start()

    load_emb.wait()
    emb_tail[...] = jnp.zeros_like(emb_tail)
    emb_tail[0:VBLOCK - VWHOLE, :] = emb[VWHOLE:VBLOCK, :]
    first_id = (s * 16 + d) * VBLOCK

    def emb_copy(k):
        return remote(looked.at[pl.ds(k * 64, 64)], arrived.at[pl.ds((2 * k + s) * 64, 64)],
                      emb_s.at[k], emb_r.at[2 * k + s], dev(1, dest(k), t))

    def is_self(k):
        return (s == 1) & (dest(k) == d)

    def is_via(k):
        return (s == 1) & ((k == VIA[0]) | (k == VIA[1]))

    def send_rows(k):
        @pl.when(is_self(k))
        def _():
            pltpu.make_async_copy(looked.at[pl.ds(k * 64, 64)], arrived.at[pl.ds((2 * k + s) * 64, 64)],
                                  emb_r.at[2 * k + s]).start()

        @pl.when(jnp.logical_not(is_self(k) | is_via(k)))
        def _():
            emb_copy(k).start()

        @pl.when(is_via(k))
        def _():
            via_copy(k // 2).start()

    def via_copy(i):
        k = 2 * i
        return remote(looked.at[pl.ds(k * 64, 64)], relay.at[i], emb_s.at[k], via_r.at[i],
                      dev(1, y * 4 + (zh + 1) % 4, t))

    def hand_on(i):
        k = VIA[i]
        return remote(relay.at[i], arrived.at[pl.ds((2 * k + 1) * 64, 64)], via_s.at[i],
                      emb_r.at[2 * k + 1], dev(1, (y + dy(k)) % 4 * 4 + (zh + 1) % 4, t))

    def look_up(i):
        for q in range(2):
            k = 2 * i + q
            pltpu.make_async_copy(ask_in.at[k], ask_in.at[k], ask_r.at[k]).wait()
            ask_col[...] = column(ask_in[k, 0:1, :])
            key_col[q * 64:(q + 1) * 64, :] = ask_col[pl.ds((d % 2) * 64, 64), :] - first_id
        want = key_col[0:LANES, :]
        hot = jnp.concatenate(
            [jnp.where(want == lane + m * LANES, 1.0, 0.0).astype(BF16) for m in range(16)], axis=1)
        rows = jnp.dot(hot[:, :VWHOLE], emb[0:VWHOLE, :], preferred_element_type=F32)
        rows += jnp.dot(hot[:, VWHOLE:], emb_tail[...], preferred_element_type=F32)
        looked[pl.ds(i * LANES, LANES), :] = rows.astype(BF16)

    def serve(i):
        look_up(i)
        send_rows(2 * i)
        send_rows(2 * i + 1)
    loop(2, serve)

    core_copy.wait()

    def x_copy(j):
        return remote(x_out.at[j - 1], x_in.at[j - 1], x_s.at[j - 1], x_r.at[j - 1],
                      dev(s, d, (x + j) % 4 * 2 + c))

    def add_core(j):
        to = (x + j) % 4
        x_out[j - 1] = (part[c, to] + core_in[to]).astype(BF16)
        x_copy(j).start()
    loop(4, add_core, 1)

    loop(EARLY // 2, serve, 2)
    loop(8, look_up, EARLY // 2)
    first_late = EARLY + s
    loop(first_late, send_rows, EARLY)

    def project_rows(i):
        h = jnp.dot(looked[pl.ds(i * 256, 256), :], basis[...], preferred_element_type=F32)
        h = h.reshape(4, 2, 32, RANK)
        pack(h[:, 0].reshape(LANES, RANK), h[:, 1].reshape(LANES, RANK), epart, pl.ds(i * LANES, LANES))
    loop(4, project_rows)
    ecore_copy = remote(epart.at[1 - c], ecore_in, ecore_s, ecore_r, partner)
    ecore_copy.start()

    @pl.when(s == 1)
    def _():
        for i in range(2):
            pltpu.make_async_copy(relay.at[i], relay.at[i], via_r.at[i]).wait()
            hand_on(i).start()

    keys[...] = route_ref[...] - route_ref[...] % TOK + pos16

    def send_column(b):
        key_col[pl.ds(b * LANES, LANES), :] = column(keys[pl.ds(b, 1), :])
    loop(16, send_column)

    def code_of(p):
        return ((p >> 6) & 1) * HALF + (p >> 7) * 64 + (p & 63)

    def send_rank(m):
        own = keys[pl.ds(m, 1), :]
        count = jnp.zeros((LANES, LANES), F32)
        for b in range(16):
            count += jnp.where(key_col[b * LANES:(b + 1) * LANES, :] < own, 1.0, 0.0)
        send_row[pl.ds(m, 1), :] = code_of(jnp.sum(count, axis=0, keepdims=True).astype(I32))
    loop(16, send_rank)

    def invert(b):
        found = jnp.zeros((LANES, LANES), I32)
        for m in range(16):
            found += jnp.where(send_row[m:m + 1, :] == sub + b * LANES, lane + m * LANES, 0)
        row = jnp.sum(found.astype(F32), axis=1, keepdims=True).astype(I32)
        send_col[pl.ds(b * LANES, LANES), :] = jnp.broadcast_to(row, (LANES, LANES))
    loop(16, invert)

    ecore_copy.wait()

    def ex_copy(j):
        to = (x + j) % 4
        return remote(ex_out.at[j - 1], ex_in.at[j - 1], ex_s.at[j - 1], ex_r.at[j - 1], dev(s, d, to * 2 + c))

    def add_ecore(j):
        to = (x + j) % 4
        ex_out[j - 1] = (epart[c, to] + ecore_in[to]).astype(BF16)
        ex_copy(j).start()
    loop(4, add_ecore, 1)

    loop(4, lambda j: x_copy(j).wait(), 1)
    mine = (part[c, x] + core_in[x] + x_in[0].astype(F32) + x_in[1].astype(F32)
            + x_in[2].astype(F32)).astype(BF16)
    gathered[x, c] = mine
    left = lax.broadcasted_iota(I32, (256, LANES), 1) < 64
    lanes256 = lax.broadcasted_iota(I32, (512, LANES), 1)

    def pick(src, places, use):
        for g in range(4):
            coefs[0:256, g * LANES:(g + 1) * LANES] = src[g * 256:(g + 1) * 256, :]

        def block(i):
            v = jnp.concatenate([places[pl.ds(i * 256, 256), :], places[pl.ds(HALF + i * 256, 256), :]], axis=0)
            low = v & 255
            hot = jnp.concatenate([jnp.where(low == lanes256 + m * LANES, 1.0, 0.0).astype(BF16)
                                   for m in range(2)], axis=1)
            rows = jnp.dot(hot, coefs[0:256, :], preferred_element_type=F32)
            which = (v >> 8) & 3
            found = rows[:, 0:LANES]
            for g in range(1, 4):
                found = jnp.where(which == g, rows[:, g * LANES:(g + 1) * LANES], found)
            other = pltpu.roll(found, 64, 1)
            second = v >= HALF
            top = jnp.where(second[0:256], other[0:256], found[0:256])
            bottom = jnp.where(second[256:512], found[256:512], other[256:512])
            use(pl.ds(i * 256, 256), jnp.where(left, top, bottom))
        loop(4, block)

    def to_slots(rows, value):
        slots[rows, :] = value.astype(BF16)
    pick(gathered.at[x, c], send_col, to_slots)

    def coef_copy(i):
        to = (d + i) % 16
        return remote(slots.at[pl.ds(to * 64, 64)], coef_in.at[pl.ds(d * 64, 64)],
                      coef_s.at[i], coef_r.at[i], dev(1 - s, to, t))
    loop(16, lambda i: coef_copy(i).start())


    loop(4, lambda j: ex_copy(j).wait(), 1)
    ebs[...] = (epart[c, x] + ecore_in[x] + ex_in[0].astype(F32) + ex_in[1].astype(F32)
                + ex_in[2].astype(F32)).astype(BF16)

    def eb_copy(k):
        return remote(ebs.at[pl.ds(k * 32, 32)], eb_in.at[pl.ds((2 * k + s) * 32, 32)],
                      eb_s.at[k], eb_r.at[2 * k + s], dev(1, dest(k), t))

    def send_eb(k):
        @pl.when(is_self(k))
        def _():
            pltpu.make_async_copy(ebs.at[pl.ds(k * 32, 32)], eb_in.at[pl.ds((2 * k + s) * 32, 32)],
                                  eb_r.at[2 * k + s]).start()

        @pl.when(jnp.logical_not(is_self(k)))
        def _():
            eb_copy(k).start()
    loop(16, send_eb)

    loop(16, send_rows, first_late)

    keys[...] = route_ref[...]
    rank_of_columns(recv_col)

    def recv_code(b):
        rows = pl.ds(b * LANES, LANES)
        recv_col[rows, :] = code_of(recv_col[rows, :])
    loop(16, recv_code)

    @pl.when(s == 1)
    def _():
        def place(b):
            p = rank_col[pl.ds(b * LANES, LANES), :]
            o = p >> 6
            to_y, to_z = (y + 4 - ((o >> 2) & 3)) & 3, (zh + 4 - (o & 3)) & 3
            odd = to_z & 1
            e = ((to_y + 1) & 3) * 2 + 1 - (to_z >> 1)
            k = jnp.where(odd == 1, 4 + to_y * 2 + (to_z >> 1), e + 8 * (e >> 2))
            code = (2 * k + (o >> 4)) * 64 + (p & 63)
            rank_col[pl.ds(b * LANES, LANES), :] = (
                ((code >> 5) & 1) * HALF + (code >> 6) * 32 + (code & 31))
            for m in range(16):
                place_e[pl.ds(b * LANES, LANES), m * LANES:(m + 1) * LANES] = (
                    jnp.where(code == lane + m * LANES, 1.0, 0.0).astype(BF16))
        loop(16, place)

    def group(g, rows):
        return jnp.dot(place_e[rows, pl.ds(pl.multiple_of(g * 512, 512), 512)],
                       arrived[pl.ds(g * 512, 512), :], preferred_element_type=F32)

    def wait_group(g):
        def one(i):
            rows = arrived.at[pl.ds(i * 64, 64)]
            pltpu.make_async_copy(rows, rows, emb_r.at[i]).wait()
        loop(g * 8 + 8, one, g * 8)

    def one_group(g):
        wait_group(g)

        def add(i):
            rows = pl.ds(i * 512, 512)
            total[rows, :] = total[rows, :] + group(g, rows)
        loop(4, add)

    @pl.when(s == 1)
    def _():
        wait_group(0)

        def first(i):
            rows = pl.ds(i * 512, 512)
            total[rows, :] = group(0, rows)
        loop(4, first)

    def coef_arrived(i):
        frm = (d + 16 - i) % 16
        rows = coef_in.at[pl.ds(frm * 64, 64)]
        pltpu.make_async_copy(rows, rows, coef_r.at[i]).wait()
    loop(16, coef_arrived)

    def put(rows, value):
        core_in[0, rows, :] = value
    pick(coef_in, recv_col, put)

    @pl.when(s == 1)
    def _():
        def eb_arrived(i):
            rows = eb_in.at[pl.ds(i * 32, 32)]
            pltpu.make_async_copy(rows, rows, eb_r.at[i]).wait()
        loop(32, eb_arrived)

        def take(rows, value):
            core_in[0, rows, :] = core_in[0, rows, :] - value
        pick(eb_in, rank_col, take)

    gathered[x, c] = core_in[0].astype(BF16)
    half_left = lax.broadcasted_iota(I32, (HALF, LANES), 1) < 64

    def ag_copy(j):
        return remote(gathered.at[x, c], gathered.at[x, c], ag_s.at[j - 1], ag_r.at[j - 1],
                      dev(s, d, (x + j) % 4 * 2 + c))

    def fwd_copy(j):
        frm = (x + 4 - j) % 4
        return remote(gathered.at[frm, c], gathered.at[frm, c], fwd_s.at[j], fwd_r.at[j], partner)

    loop(4, lambda j: ag_copy(j).start(), 1)
    fwd_copy(0).start()

    @pl.when(s == 1)
    def _():
        one_group(1)

    def forward(j):
        frm = (x + 4 - j) % 4
        pltpu.make_async_copy(gathered.at[frm, c], gathered.at[frm, c], ag_r.at[j - 1]).wait()
        fwd_copy(j).start()
    loop(4, forward, 1)

    @pl.when(s == 1)
    def _():
        one_group(2)

    def from_partner(j):
        frm = (x + 4 - j) % 4
        pltpu.make_async_copy(gathered.at[frm, 1 - c], gathered.at[frm, 1 - c], fwd_r.at[j]).wait()
    loop(4, from_partner)
    for g in range(4):
        a, b = gathered[g, 0].astype(F32), gathered[g, 1].astype(F32)
        cols = slice(g * LANES, (g + 1) * LANES)
        coefs[0:HALF, cols] = jnp.where(half_left, a, pltpu.roll(b, 64, 1)).astype(BF16)
        coefs[HALF:TOK, cols] = jnp.where(half_left, pltpu.roll(a, 64, 1), b).astype(BF16)

    def lifted(rows):
        return lax.dot_general(
            coefs[rows, :], basis[...], (((1,), (1,)), ((), ())), preferred_element_type=F32)

    @pl.when(s == 0)
    def _():
        def finish(i):
            rows = pl.ds(i * 512, 512)
            acts[rows, :] = lifted(rows).astype(BF16)
        loop(4, finish)

    @pl.when(s == 1)
    def _():
        def lift(i):
            rows = pl.ds(i * 512, 512)
            total[rows, :] = total[rows, :] + lifted(rows)
        loop(4, lift)
        wait_group(3)

        def finish(i):
            rows = pl.ds(i * 512, 512)
            acts[rows, :] = (total[rows, :] + group(3, rows)).astype(BF16)
        loop(4, finish)

    @pl.when(s == 1)
    def _():
        def asked(i):
            k, so = i // 2, i % 2

            @pl.when((so != 1) | (source(k) != d))
            def _():
                remote(ask.at[0], ask_in.at[0], ask_s.at[i], ask_r.at[0], partner).wait_send()
        loop(32, asked)

    def sent(k):
        coef_copy(k).wait_send()

        @pl.when(jnp.logical_not(is_self(k)))
        def _():
            emb_copy(k).wait_send()
            eb_copy(k).wait_send()
    loop(16, sent)

    @pl.when(s == 1)
    def _():
        hand_on(0).wait_send()
        hand_on(1).wait_send()
    loop(4, lambda j: ag_copy(j).wait_send(), 1)
    loop(4, lambda j: fwd_copy(j).wait_send())


def on_device(outgoing, embedding, shared_basis, token_ids, row_route):
    any_ = pl.BlockSpec(memory_space=pl.ANY)
    vmem = pl.BlockSpec(memory_space=pltpu.VMEM)
    V, D = pltpu.VMEM, pltpu.SemaphoreType.DMA
    scratch = [
        V((VBLOCK, FEAT), BF16), V((LANES, FEAT), BF16), V((FEAT, RANK), BF16),
        V((HALF, FEAT), BF16), V((TOK, FEAT), BF16), V((TOK, FEAT), F32), V((TOK, TOK), BF16),
        V((16, LANES), I32), V((TOK, LANES), I32), V((TOK, LANES), I32), V((TOK, LANES), I32), V((TOK, LANES), I32),
        V((16, LANES), I32), V((16, 8, LANES), I32), V((16, 8, LANES), I32), V((LANES, LANES), I32),
        V((2, 64, FEAT), BF16),
        V((2, 4, HALF, LANES), F32), V((4, HALF, LANES), F32), V((3, HALF, LANES), BF16), V((3, HALF, LANES), BF16),
        V((2, 4, 512, LANES), F32), V((4, 512, LANES), F32), V((3, 512, LANES), BF16), V((3, 512, LANES), BF16),
        V((HALF, LANES), BF16), V((HALF, LANES), BF16), V((512, LANES), BF16), V((HALF, LANES), BF16),
        V((4, 2, HALF, LANES), BF16), V((TOK, RANK), BF16),
        D((3,)), D((32,)), D((16,)), D((16,)), D((32,)), D((2,)), D((2,)), D, D, D((3,)), D((3,)),
        D, D, D((3,)), D((3,)), D((16,)), D((16,)), D((16,)), D((32,)),
        D((3,)), D((3,)), D((4,)), D((4,)),
    ]
    out = pl.pallas_call(
        kernel,
        out_shape=pltpu.VMEM((TOK, FEAT), BF16),
        in_specs=[any_, any_, any_, vmem, vmem],
        out_specs=vmem,
        scratch_shapes=scratch,
        compiler_params=pltpu.CompilerParams(
            collective_id=0, has_side_effects=True, vmem_limit_bytes=57 * 1024 * 1024),
    )(outgoing[0], embedding, shared_basis,
      token_ids.reshape(16, LANES), row_route.reshape(16, LANES))
    return out[None]


def solution(mesh):
    return jax.shard_map(
        on_device,
        mesh=mesh,
        in_specs=(
            P("section", "dp", "tensor"),
            P(("section", "dp"), "tensor"),
            P("tensor", None),
            P("section", "dp"),
            P("section", "dp"),
        ),
        out_specs=P("section", "dp", "tensor"),
        check_vma=False,
    )
```
